256 devices in a mesh: rep: 16 (over y_lo, z), fsdp: 16 (over y_hi, x, core).
Axes of the slice: x: 4, y: 4 (y_hi: 2, y_lo: 2; y = y_hi * 2 + y_lo), z: 8, core: 2. Of those that a mesh axis runs over, the one named last changes fastest.
Arguments:
- outer_weights: bfloat16 [8192, 1024], P('fsdp'), may hold values from -4 to 4
- inner_weights: bfloat16 [16, 8192, 1024], P('rep', 'fsdp'), may hold values from -10 to 10
- momentum: float32 [8192, 1024], P('fsdp'), may hold values from -1.2 to 1.2
- tokens: bfloat16 [16, 8192, 8192], P('rep', 'fsdp'), may hold values from -6 to 6
Outputs:
- outer_next: bfloat16 [8192, 1024], P('fsdp')
- momentum_next: float32 [8192, 1024], P('fsdp')
- keys: bfloat16 [16, 8192, 1024], P('rep', 'fsdp')
The draws below stay inside these ranges and needn't reach their ends.
All inputs are finite; a program needn't handle non-finite values. Where the reference program divides by a largest or mean magnitude, that divisor is 1e-20 or more.
Results may differ from the reference program's by a relative error of at most 0.015.
Values may be sent and summed in bfloat16 or wider, within the bound.
No kernel may reach another device: no remote copies, remote signals or barrier semaphores. Data moves between devices by JAX's collectives and lax.ppermute only.
A program may use at most 128 MiB of HBM per device.

```python
import jax
import jax.numpy as jnp
from jax import lax

D = 8192
KV = 1024
REP = 16
TOK = 8192


def shared_base(key):
    return jnp.clip(jax.random.normal(key, (D, KV), jnp.float32), -4.0, 4.0)


def draw_outer_weights(key, part):
    base = shared_base(key)
    return base.astype(jnp.bfloat16)


def draw_inner_weights(key, part):
    base = shared_base(key)
    key = jax.random.fold_in(key, 3)
    key_noise, key_rows = jax.random.split(key, 2)
    row_scale = jnp.exp(jax.random.uniform(key_rows, (REP, D, 1), jnp.float32, jnp.log(0.3), jnp.log(3.0)))
    noise = jnp.clip(jax.random.normal(key_noise, (REP, D, KV), jnp.float32), -4.0, 4.0)
    drift = 0.5 * noise * row_scale
    outer = base.astype(jnp.bfloat16).astype(jnp.float32)
    return (outer[None] - drift).astype(jnp.bfloat16)


def levels(stream_key, dims, pieces, low, top_value):
    loudness = 1.0
    for axis_at, blocks in pieces:
        draws = jax.random.uniform(jax.random.fold_in(jax.random.fold_in(stream_key, 6), axis_at), (blocks,), jnp.float32, low / len(pieces), top_value / len(pieces))
        loudness = loudness * jnp.repeat(jnp.exp(draws), dims[axis_at] // blocks).reshape((-1,) + (1,) * (len(dims) - 1 - axis_at))
    return loudness


def scatter_about(own_key, dims, scale, reach, cuts=(), kind=jnp.bfloat16):
    loudness = levels(own_key, dims, cuts, -0.22, 0.18) if cuts else 1.0
    entries = jax.random.normal(own_key, dims, jnp.float32) * scale * loudness
    return jnp.minimum(jnp.maximum(entries, -reach), reach).astype(kind)


def setup_inputs(seed: int = 0) -> dict:
    key_list = jax.random.split(jax.random.key(seed), 5)
    outer_weights = draw_outer_weights(jax.random.fold_in(key_list[4], 71), 0)
    inner_weights = draw_inner_weights(jax.random.fold_in(key_list[4], 71), 0)
    momentum = scatter_about(key_list[2], (D, KV), 0.2, 1.2, ((0, 16),), jnp.float32)
    tokens = scatter_about(key_list[3], (REP, TOK, D), 1.0, 6.0, ((0, 16), (1, 16)))
    return {"outer_weights": outer_weights, "inner_weights": inner_weights, "momentum": momentum, "tokens": tokens}


def dequantized(outer_weights, inner_one):
    delta = outer_weights.astype(jnp.float32) - inner_one.astype(jnp.float32)
    rows = delta.shape[0]
    blocks = delta.reshape(rows, delta.shape[1] // 128, 128)
    scale = jnp.max(jnp.abs(blocks), axis=2, keepdims=True) + 1e-6
    quant = (blocks / scale).astype(jnp.bfloat16)
    quant = lax.optimization_barrier(quant)
    return (quant.astype(jnp.float32) * scale).reshape(rows, delta.shape[1])


def reference(outer_weights, inner_weights, momentum, tokens):
    def add_term(total, inner_one):
        return total + dequantized(outer_weights, inner_one), None

    total, _ = lax.scan(add_term, jnp.zeros(outer_weights.shape, jnp.float32), inner_weights)
    average = total / REP
    momentum_next = 0.9 * momentum + average
    outer_next = (outer_weights.astype(jnp.float32) - 0.7 * (average + 0.9 * momentum_next)).astype(jnp.bfloat16)

    def forward(pair):
        inner_one, token_rows = pair
        mixed = (0.5 * inner_one.astype(jnp.float32) + 0.5 * outer_next.astype(jnp.float32)).astype(jnp.bfloat16)
        summed = jnp.dot(token_rows, mixed, preferred_element_type=jnp.float32)
        return (summed * (D ** -0.5)).astype(jnp.bfloat16)

    keys = lax.map(forward, (inner_weights, tokens))
    return outer_next, momentum_next, keys
```

```python
import jax
import jax.numpy as jnp
from jax import lax
from jax.experimental import pallas as pl
from jax.experimental.pallas import tpu as pltpu
from jax.sharding import PartitionSpec as P

YH, X, CORE = 2, 4, 2
REP = 16
GROUPS = ((0, 256), (256, 256), (512, 256), (768, 256))
MIB = 1 << 20


def fsdp_move(array, dy=0, dx=0, dc=0):
    perm = []
    for y in range(YH):
        for x in range(X):
            for c in range(CORE):
                to = (((y + dy) % YH) * X + (x + dx) % X) * CORE + (c + dc) % CORE
                perm.append(((y * X + x) * CORE + c, to))
    return lax.ppermute(array, "fsdp", perm)


def average_kernel(recv_ref, outer_ref, out_ref):
    replicas, rows, width = recv_ref.shape
    for at in range(0, width, 128):
        cols = slice(at, at + 128)
        outer = outer_ref[:, cols].astype(jnp.float32)
        total = jnp.zeros((rows, 128), jnp.float32)
        for r in range(replicas):
            delta = outer - recv_ref[r, :, cols].astype(jnp.float32)
            scale = jnp.max(jnp.abs(delta), axis=1, keepdims=True) + 1e-6
            quant = (delta / scale).astype(jnp.bfloat16)
            total = total + quant.astype(jnp.float32) * scale
        out_ref[:, cols] = (total / replicas).astype(out_ref.dtype)


def average_slice(recv, outer_rows):
    replicas, rows, width = recv.shape
    return pl.pallas_call(
        average_kernel,
        out_shape=jax.ShapeDtypeStruct((rows, width), jnp.bfloat16),
        cost_estimate=pl.CostEstimate(
            flops=10 * replicas * rows * width, bytes_accessed=2 * replicas * rows * width, transcendentals=0
        ),
        name="average_slice",
    )(recv, outer_rows)


def pick_kernel(at_ref, in_ref, out_ref):
    out_ref[...] = in_ref[...]


def pick_columns(array, blocks, wide):
    rows = array.shape[0]
    count = blocks.shape[0]
    return pl.pallas_call(
        pick_kernel,
        grid_spec=pltpu.PrefetchScalarGridSpec(
            num_scalar_prefetch=1,
            grid=(count,),
            in_specs=[pl.BlockSpec((rows, wide), lambda k, at: (0, at[k]))],
            out_specs=pl.BlockSpec((rows, wide), lambda k, at: (0, k)),
        ),
        out_shape=jax.ShapeDtypeStruct((rows, count * wide), array.dtype),
        cost_estimate=pl.CostEstimate(flops=0, bytes_accessed=4 * rows * count * wide, transcendentals=0),
        name="pick_columns",
    )(blocks, array)


def blocks_dot(array, blocks, pieces):
    rows = array.shape[0]
    tile = 256
    wide = sum(p.shape[0] for p in pieces[0])
    width = pieces[0][0].shape[1]
    flat = [p for piece in pieces for p in piece]
    count = len(pieces)

    def kernel(at_ref, *refs):
        lefts, rights, out_ref = refs[:count], refs[count:-1], refs[-1]
        total = jnp.zeros(out_ref.shape, jnp.float32)
        i = 0
        for k in range(count):
            at = 0
            for p in pieces[k]:
                total = total + jnp.dot(
                    lefts[k][:, at : at + p.shape[0]], rights[i][...], preferred_element_type=jnp.float32
                )
                at += p.shape[0]
                i += 1
        out_ref[...] = total

    def left_spec(k):
        return pl.BlockSpec((tile, wide), lambda i, at: (i, at[k]))

    return pl.pallas_call(
        kernel,
        grid_spec=pltpu.PrefetchScalarGridSpec(
            num_scalar_prefetch=1,
            grid=(rows // tile,),
            in_specs=[left_spec(k) for k in range(count)]
            + [pl.BlockSpec(p.shape, lambda i, at: (0, 0)) for p in flat],
            out_specs=pl.BlockSpec((tile, width), lambda i, at: (i, 0)),
        ),
        out_shape=jax.ShapeDtypeStruct((rows, width), jnp.float32),
        compiler_params=pltpu.CompilerParams(vmem_limit_bytes=48 * MIB),
        cost_estimate=pl.CostEstimate(
            flops=2 * rows * wide * count * width,
            bytes_accessed=2 * wide * count * (rows + width) + 4 * rows * width,
            transcendentals=0,
        ),
        name="blocks_dot",
    )(blocks, *([array] * count), *flat)


def gather_blocks(mine):
    half = mine.shape[0] // 2
    there = fsdp_move(mine, dy=1)
    found = []
    for block in (mine, there):
        from_left = fsdp_move(block, dx=1)
        from_right = fsdp_move(block, dx=-1)
        top = fsdp_move(from_left[:half], dx=1)
        bottom = fsdp_move(from_right[half:], dx=-1)
        found += [[block], [from_left], [from_right], [top, bottom]]
    return found


def chip_order():
    chip = lax.axis_index("fsdp") // CORE
    y, x = chip // X, chip % X
    order = []
    for dy in range(YH):
        for dx in (0, X - 1, 1, 2):
            order.append(((y + dy) % YH) * X + (x + dx) % X)
    return jnp.stack(order).astype(jnp.int32)


def shards(outer_weights, inner_weights, momentum, tokens):
    inner = inner_weights[0]
    token_rows = tokens[0]
    rows = inner.shape[0]
    part = rows // REP
    rep = lax.axis_index("rep")
    core = lax.axis_index("fsdp") % CORE
    chips = chip_order()
    width = token_rows.shape[1]

    other_tokens = fsdp_move(
        pick_columns(token_rows, 2 * jnp.arange(YH * X, dtype=jnp.int32) + 1 - core, rows), dc=1
    )
    outer_nexts, momentum_nexts, keys = [], [], []
    for at, wide in GROUPS:
        inner_g = inner[:, at : at + wide]
        outer_g = outer_weights[:, at : at + wide]
        recv = lax.all_to_all(inner_g.reshape(REP, part, wide), "rep", 0, 0)
        mean = average_slice(recv, lax.dynamic_slice(outer_weights, (rep * part, at), (part, wide)))
        average = lax.all_to_all(jnp.broadcast_to(mean[None], (REP, part, wide)), "rep", 0, 0)
        average = average.reshape(rows, wide).astype(jnp.float32)
        momentum_next = 0.9 * momentum[:, at : at + wide] + average
        outer_next = (outer_g.astype(jnp.float32) - 0.7 * (average + 0.9 * momentum_next)).astype(jnp.bfloat16)
        mixed = (0.5 * inner_g.astype(jnp.float32) + 0.5 * outer_next.astype(jnp.float32)).astype(jnp.bfloat16)
        pieces = gather_blocks(mixed)
        theirs = fsdp_move(blocks_dot(other_tokens, chips, pieces), dc=1)
        ours = blocks_dot(token_rows, 2 * chips + core, pieces)
        keys.append(((ours + theirs) * width ** (-0.5)).astype(jnp.bfloat16))
        outer_nexts.append(outer_next)
        momentum_nexts.append(momentum_next)
    return (
        jnp.concatenate(outer_nexts, axis=1),
        jnp.concatenate(momentum_nexts, axis=1),
        jnp.concatenate(keys, axis=1)[None],
    )


def solution(mesh):
    placed = (P("fsdp", None), P("rep", "fsdp", None), P("fsdp", None), P("rep", "fsdp", None))
    return jax.shard_map(
        shards,
        mesh=mesh,
        in_specs=placed,
        out_specs=(P("fsdp", None), P("fsdp", None), P("rep", "fsdp", None)),
        check_vma=False,
    )
```

```python
import jax
import jax.numpy as jnp
from jax import lax
from jax.experimental import pallas as pl
from jax.experimental.pallas import tpu as pltpu
from jax.sharding import PartitionSpec as P

YH, X, CORE = 2, 4, 2
CHIPS = YH * X
REP = 16
MAIN, EARLY_WIDE = 768, 256
NEAR = ((0, 0), (0, -1), (0, 1), (1, 0))
SIDES = ((1, -1), (1, 1))
LAST = ((0, 2), (1, 2))
ORDER = tuple((dy, dx) for dx in (0, -1, 1, 2) for dy in range(YH))
MIB = 1 << 20
F32, BF16 = jnp.float32, jnp.bfloat16
YL, Z = 2, 8
SAME_YL = [[yl * Z + z for z in range(Z)] for yl in range(YL)]


def fsdp_move(array, dy=0, dx=0, dc=0):
    perm = []
    for y in range(YH):
        for x in range(X):
            for c in range(CORE):
                to = (((y + dy) % YH) * X + (x + dx) % X) * CORE + (c + dc) % CORE
                perm.append(((y * X + x) * CORE + c, to))
    return lax.ppermute(array, "fsdp", perm)


def swap_yl(array):
    return lax.ppermute(array, "rep", [(r, (r + Z) % REP) for r in range(REP)])


def to_all_replicas(array):
    return lax.all_to_all(jnp.broadcast_to(array[None], (REP, *array.shape)), "rep", 0, 0)


def to_all_z(array):
    return lax.all_to_all(
        jnp.broadcast_to(array[None], (Z, *array.shape)), "rep", 0, 0, axis_index_groups=SAME_YL
    )


def after(array, *others):
    def kernel(*refs):
        pass

    space = pl.BlockSpec(memory_space=pl.ANY)
    return pl.pallas_call(
        kernel,
        in_specs=[space] * (1 + len(others)),
        out_specs=space,
        out_shape=jax.ShapeDtypeStruct(array.shape, array.dtype),
        input_output_aliases={0: 0},
        name="after",
    )(array, *others)


def update(outer, moment, average):
    momentum_next = 0.9 * moment + average
    return (outer.astype(F32) - 0.7 * (average + 0.9 * momentum_next)).astype(BF16), momentum_next


def average_slice(recv, outer_rows, momentum_rows):
    replicas, rows, columns = recv.shape

    def kernel(recv_ref, outer_ref, momentum_ref, copies_ref, early_ref, mean_ref):
        for first in range(0, columns, 128):
            cols = slice(first, first + 128)
            outer = outer_ref[:, cols].astype(F32)
            total = jnp.zeros((rows, 128), F32)
            for r in range(replicas):
                delta = outer - recv_ref[r, :, cols].astype(F32)
                scale = jnp.max(jnp.abs(delta), axis=1, keepdims=True) + 1e-6
                quant = (delta / scale).astype(BF16)
                total = total + quant.astype(F32) * scale
            mean = total / replicas
            if first < MAIN:
                for r in range(replicas):
                    copies_ref[r, :, cols] = mean.astype(BF16)
            else:
                cols = slice(first - MAIN, first - MAIN + 128)
                mean_ref[:, cols] = mean.astype(BF16)
                early_ref[:, cols] = update(outer, momentum_ref[:, cols], mean)[0]

    return pl.pallas_call(
        kernel,
        out_shape=[
            jax.ShapeDtypeStruct((replicas, rows, MAIN), BF16),
            jax.ShapeDtypeStruct((rows, columns - MAIN), BF16),
            jax.ShapeDtypeStruct((rows, columns - MAIN), BF16),
        ],
        cost_estimate=pl.CostEstimate(
            flops=10 * replicas * rows * columns, bytes_accessed=4 * replicas * rows * columns, transcendentals=0
        ),
        name="average_slice",
    )(recv, outer_rows, momentum_rows)


def mix(one, other):
    return (0.5 * one.astype(F32) + 0.5 * other.astype(F32)).astype(BF16)


def mix_early(inners, late, yl):
    count, (rows, wide) = len(inners), inners[0].shape
    half = rows // YL

    def kernel(yl_ref, *refs):
        mixed_ref, outer_ref, average_ref = refs[-3:]
        lates = refs[count:-3]
        for h in range(YL):
            at = slice(h * half, h * half + half)
            outers = [r[...].reshape(half, wide) for r in lates[h * (count + 1) : (h + 1) * (count + 1)]]
            for k in range(count):
                mixed_ref[k, at] = mix(refs[k][at], outers[k])
            outer_ref[at] = outers[0]
            average_ref[at] = outers[count]

    def late_spec(h, k):
        return pl.BlockSpec((Z, None, None, rows // REP, wide), lambda i, yl: (0, (yl[0] + h) % YL, k, 0, 0))

    def whole(*shape):
        return pl.BlockSpec(shape, lambda i, yl: (0,) * len(shape))

    lates = [late_spec(h, k) for h in range(YL) for k in range(count + 1)]
    return pl.pallas_call(
        kernel,
        grid_spec=pltpu.PrefetchScalarGridSpec(
            num_scalar_prefetch=1,
            grid=(1,),
            in_specs=[whole(rows, wide)] * count + lates,
            out_specs=[whole(count, rows, wide), whole(rows, wide), whole(rows, wide)],
        ),
        out_shape=[
            jax.ShapeDtypeStruct((count, rows, wide), BF16),
            jax.ShapeDtypeStruct((rows, wide), BF16),
            jax.ShapeDtypeStruct((rows, wide), BF16),
        ],
        compiler_params=pltpu.CompilerParams(vmem_limit_bytes=48 * MIB),
        cost_estimate=pl.CostEstimate(
            flops=3 * count * rows * wide, bytes_accessed=6 * count * rows * wide, transcendentals=0
        ),
        name="mix_early",
    )(yl[None], *inners, *([late] * len(lates)))


def blocks_dot(lefts, blocks, pieces, start=None):
    rows, tile = lefts[0].shape[0], 256
    steps = rows // tile
    count, sides = len(pieces), len(lefts)
    arrays = []
    for piece in pieces:
        if not any(piece[0] is a for a in arrays):
            arrays.append(piece[0])
    found = [next(i for i, a in enumerate(arrays) if a is piece[0]) for piece in pieces]
    deep, width = arrays[0].shape[-2:]
    added = list(start) if start else []

    def kernel(at_ref, *refs):
        rights = refs[sides * count : sides * count + len(arrays)]
        starts = refs[sides * count + len(arrays) : -sides]
        step = pl.program_id(0)
        for side in range(sides):

            @pl.when(step // steps == side)
            def _(side=side):
                total = starts[side][...] if starts else jnp.zeros((tile, width), F32)
                for k, piece in enumerate(pieces):
                    right = rights[found[k]]
                    right = right[piece[1]] if len(piece) > 1 else right[...]
                    total = total + jnp.dot(refs[side * count + k][...], right, preferred_element_type=F32)
                refs[side - sides][...] = total

    def row(side, i):
        return jnp.clip(i - side * steps, 0, steps - 1)

    def left_spec(side, k):
        return pl.BlockSpec((tile, deep), lambda i, at: (row(side, i), at[k]))

    def row_spec(side):
        return pl.BlockSpec((tile, width), lambda i, at: (row(side, i), 0))

    def whole(array):
        return pl.BlockSpec(array.shape, lambda i, at: (0,) * array.ndim)

    return list(
        pl.pallas_call(
            kernel,
            grid_spec=pltpu.PrefetchScalarGridSpec(
                num_scalar_prefetch=1,
                grid=(sides * steps,),
                in_specs=[left_spec(side, k) for side in range(sides) for k in range(count)]
                + [whole(a) for a in arrays]
                + [row_spec(side) for side in range(len(added))],
                out_specs=[row_spec(side) for side in range(sides)],
            ),
            out_shape=[jax.ShapeDtypeStruct((rows, width), F32)] * sides,
            compiler_params=pltpu.CompilerParams(vmem_limit_bytes=48 * MIB),
            cost_estimate=pl.CostEstimate(
                flops=2 * sides * rows * deep * count * width,
                bytes_accessed=2 * deep * count * (sides * rows + width) + 4 * sides * rows * width,
                transcendentals=0,
            ),
            name="blocks_dot",
        )(blocks, *[left for left in lefts for _ in range(count)], *arrays, *added)
    )


def shards(outer_weights, inner_weights, momentum, tokens):
    inner = inner_weights[0]
    token_rows = tokens[0]
    rows, columns = inner.shape
    part = rows // REP
    rep = lax.axis_index("rep")
    core = lax.axis_index("fsdp") % CORE
    chip = lax.axis_index("fsdp") // CORE
    y, x = chip // X, chip % X
    width = token_rows.shape[1]

    def chips_of(moves):
        return jnp.stack([((y + dy) % YH) * X + (x + dx) % X for dy, dx in moves]).astype(jnp.int32)

    early = slice(MAIN, MAIN + EARLY_WIDE)
    yl = (rep // Z).astype(jnp.int32)

    recv = lax.all_to_all(inner.reshape(REP, part, columns), "rep", 0, 0)
    their_tokens = fsdp_move(token_rows, dc=1)
    mine = inner[:, early]
    there, left, right, across = (fsdp_move(mine, *to) for to in ((1, 0), (0, 1), (0, -1), (0, 2)))
    outer_part = lax.dynamic_slice(outer_weights, (rep * part, 0), (part, columns))
    outer_part = after(outer_part, their_tokens, there, left, right, across)
    momentum_part = lax.dynamic_slice(momentum, (rep * part, MAIN), (part, EARLY_WIDE))
    copies, outer_slice, mean = average_slice(recv, outer_part, momentum_part)
    average = lax.all_to_all(copies, "rep", 0, 0).reshape(rows, MAIN)

    there_left, there_right, there_across = (fsdp_move(there, 0, dx) for dx in (1, -1, 2))
    inners = [mine, there, left, there_left, right, there_right, across, there_across]
    pair = jnp.stack([outer_slice, fsdp_move(outer_slice, dy=1)])
    slices = jnp.concatenate(
        [pair, fsdp_move(pair, dx=1), fsdp_move(pair, dx=-1), fsdp_move(pair, dx=2), mean[None]]
    )
    slices = jnp.stack([slices, swap_yl(slices)])
    average = after(average, there_left, there_right, there_across)
    mixed = mix(
        inner[:, :MAIN], update(outer_weights[:, :MAIN], momentum[:, :MAIN], average.astype(F32))[0]
    )
    late = to_all_z(after(slices, mixed))

    both = [their_tokens, token_rows]

    def dot(chips, pieces, start=None, lefts=both):
        return blocks_dot(lefts, CORE * chips_of(chips) + core, pieces, start)

    left, right, there = fsdp_move(mixed, dx=1), fsdp_move(mixed, dx=-1), fsdp_move(mixed, dy=1)
    there_left, there_right, across = fsdp_move(there, dx=1), fsdp_move(there, dx=-1), fsdp_move(left, dx=1)
    sums = dot(NEAR, [(mixed,), (left,), (right,), (there,)])
    there_right = after(there_right, sums[0])
    there_across = fsdp_move(there_right, dx=-1)
    sums = dot(SIDES, [(there_left,), (there_right,)], sums)

    mixed_early, outer_early, average_early = mix_early(inners, after(late, sums[0]), yl)
    sums_early = dot(ORDER, [(mixed_early, k) for k in range(CHIPS)])
    theirs_early = fsdp_move(sums_early[0], dc=1)
    outer_main, momentum_main = update(
        outer_weights[:, :MAIN], momentum[:, :MAIN], after(average, there_right).astype(F32)
    )
    momentum_early = 0.9 * momentum[:, early] + average_early.astype(F32)
    outer_next = jnp.concatenate([outer_main, outer_early], axis=1)
    momentum_next = jnp.concatenate([momentum_main, momentum_early], axis=1)

    last = [(across,), (there_across,)]
    theirs = fsdp_move(dot(LAST, last, sums[:1], both[:1])[0], dc=1)
    ours = dot(LAST, last, sums[1:], both[1:])[0]
    keys = jnp.concatenate([ours + theirs, sums_early[1] + theirs_early], axis=1) * width ** (-0.5)
    return outer_next, momentum_next, keys.astype(BF16)[None]


def solution(mesh):
    placed = (P("fsdp", None), P("rep", "fsdp", None), P("fsdp", None), P("rep", "fsdp", None))
    return jax.shard_map(
        shards,
        mesh=mesh,
        in_specs=placed,
        out_specs=(P("fsdp", None), P("fsdp", None), P("rep", "fsdp", None)),
        check_vma=False,
    )
```

```python
import jax
import jax.numpy as jnp
from jax import lax
from jax.experimental import pallas as pl
from jax.experimental.pallas import tpu as pltpu
from jax.sharding import PartitionSpec as P

YH, X, CORE = 2, 4, 2
CHIPS = YH * X
REP = 16
MAIN, EARLY_WIDE = 768, 256
NEAR = ((0, 0), (0, -1), (0, 1), (1, 0))
SIDES = ((1, -1), (1, 1))
LAST = ((0, 2), (1, 2))
ORDER = tuple((dy, dx) for dx in (0, -1, 1, 2) for dy in range(YH))
MIB = 1 << 20
F32, BF16 = jnp.float32, jnp.bfloat16
YL, Z = 2, 8
SAME_YL = [[yl * Z + z for z in range(Z)] for yl in range(YL)]


def fsdp_move(array, dy=0, dx=0, dc=0):
    perm = []
    for y in range(YH):
        for x in range(X):
            for c in range(CORE):
                to = (((y + dy) % YH) * X + (x + dx) % X) * CORE + (c + dc) % CORE
                perm.append(((y * X + x) * CORE + c, to))
    return lax.ppermute(array, "fsdp", perm)


def swap_yl(array):
    return lax.ppermute(array, "rep", [(r, (r + Z) % REP) for r in range(REP)])


def to_all_replicas(array):
    return lax.all_to_all(jnp.broadcast_to(array[None], (REP, *array.shape)), "rep", 0, 0)


def after(array, *others):
    def kernel(*refs):
        pass

    space = pl.BlockSpec(memory_space=pl.ANY)
    return pl.pallas_call(
        kernel,
        in_specs=[space] * (1 + len(others)),
        out_specs=space,
        out_shape=jax.ShapeDtypeStruct(array.shape, array.dtype),
        input_output_aliases={0: 0},
        name="after",
    )(array, *others)


def update(outer, moment, average):
    momentum_next = 0.9 * moment + average
    return (outer.astype(F32) - 0.7 * (average + 0.9 * momentum_next)).astype(BF16), momentum_next


def average_slice(recv, outer_rows, momentum_rows):
    replicas, rows, columns = recv.shape

    def kernel(recv_ref, outer_ref, momentum_ref, copies_ref, early_ref, mean_ref):
        for first in range(0, columns, 128):
            cols = slice(first, first + 128)
            outer = outer_ref[:, cols].astype(F32)
            total = jnp.zeros((rows, 128), F32)
            for r in range(replicas):
                delta = outer - recv_ref[r, :, cols].astype(F32)
                scale = jnp.max(jnp.abs(delta), axis=1, keepdims=True) + 1e-6
                quant = (delta / scale).astype(BF16)
                total = total + quant.astype(F32) * scale
            mean = total / replicas
            if first < MAIN:
                for r in range(replicas):
                    copies_ref[r, :, cols] = mean.astype(BF16)
            else:
                cols = slice(first - MAIN, first - MAIN + 128)
                mean_ref[:, cols] = mean.astype(BF16)
                early_ref[:, cols] = update(outer, momentum_ref[:, cols], mean)[0]

    return pl.pallas_call(
        kernel,
        out_shape=[
            jax.ShapeDtypeStruct((replicas, rows, MAIN), BF16),
            jax.ShapeDtypeStruct((rows, columns - MAIN), BF16),
            jax.ShapeDtypeStruct((rows, columns - MAIN), BF16),
        ],
        cost_estimate=pl.CostEstimate(
            flops=10 * replicas * rows * columns, bytes_accessed=4 * replicas * rows * columns, transcendentals=0
        ),
        name="average_slice",
    )(recv, outer_rows, momentum_rows)


def mix(one, other):
    return (0.5 * one.astype(F32) + 0.5 * other.astype(F32)).astype(BF16)


def mix_early(inners, late, yl):
    count, (rows, wide) = len(inners), inners[0].shape
    half = rows // YL

    def kernel(yl_ref, *refs):
        mixed_ref, outer_ref, average_ref = refs[-3:]
        lates = refs[count:-3]
        for h in range(YL):
            at = slice(h * half, h * half + half)
            outers = [r[...].reshape(half, wide) for r in lates[h * (count + 1) : (h + 1) * (count + 1)]]
            for k in range(count):
                mixed_ref[k, at] = mix(refs[k][at], outers[k])
            outer_ref[at] = outers[0]
            average_ref[at] = outers[count]

    def late_spec(h, k):
        return pl.BlockSpec((Z, None, None, rows // REP, wide), lambda i, yl: (0, (yl[0] + h) % YL, k, 0, 0))

    def whole(*shape):
        return pl.BlockSpec(shape, lambda i, yl: (0,) * len(shape))

    lates = [late_spec(h, k) for h in range(YL) for k in range(count + 1)]
    return pl.pallas_call(
        kernel,
        grid_spec=pltpu.PrefetchScalarGridSpec(
            num_scalar_prefetch=1,
            grid=(1,),
            in_specs=[whole(rows, wide)] * count + lates,
            out_specs=[whole(count, rows, wide), whole(rows, wide), whole(rows, wide)],
        ),
        out_shape=[
            jax.ShapeDtypeStruct((count, rows, wide), BF16),
            jax.ShapeDtypeStruct((rows, wide), BF16),
            jax.ShapeDtypeStruct((rows, wide), BF16),
        ],
        compiler_params=pltpu.CompilerParams(vmem_limit_bytes=60 * MIB),
        cost_estimate=pl.CostEstimate(
            flops=3 * count * rows * wide, bytes_accessed=6 * count * rows * wide, transcendentals=0
        ),
        name="mix_early",
    )(yl[None], *inners, *([late] * len(lates)))


def blocks_dot(lefts, blocks, pieces, start=None, out=F32):
    rows, tile = lefts[0].shape[0], 256
    steps = rows // tile
    count, sides = len(pieces), len(lefts)
    arrays = []
    for piece in pieces:
        if not any(piece[0] is a for a in arrays):
            arrays.append(piece[0])
    found = [next(i for i, a in enumerate(arrays) if a is piece[0]) for piece in pieces]
    deep, width = arrays[0].shape[-2:]
    added = list(start) if start else []

    def kernel(at_ref, *refs):
        rights = refs[sides * count : sides * count + len(arrays)]
        starts = refs[sides * count + len(arrays) : -sides]
        step = pl.program_id(0)
        for side in range(sides):

            @pl.when(step // steps == side)
            def _(side=side):
                total = starts[side][...] if starts else jnp.zeros((tile, width), F32)
                for k, piece in enumerate(pieces):
                    right = rights[found[k]]
                    right = right[piece[1]] if len(piece) > 1 else right[...]
                    total = total + jnp.dot(refs[side * count + k][...], right, preferred_element_type=F32)
                refs[side - sides][...] = total.astype(out)

    def row(side, i):
        return jnp.clip(i - side * steps, 0, steps - 1)

    def left_spec(side, k):
        return pl.BlockSpec((tile, deep), lambda i, at: (row(side, i), at[k]))

    def row_spec(side):
        return pl.BlockSpec((tile, width), lambda i, at: (row(side, i), 0))

    def whole(array):
        return pl.BlockSpec(array.shape, lambda i, at: (0,) * array.ndim)

    return list(
        pl.pallas_call(
            kernel,
            grid_spec=pltpu.PrefetchScalarGridSpec(
                num_scalar_prefetch=1,
                grid=(sides * steps,),
                in_specs=[left_spec(side, k) for side in range(sides) for k in range(count)]
                + [whole(a) for a in arrays]
                + [row_spec(side) for side in range(len(added))],
                out_specs=[row_spec(side) for side in range(sides)],
            ),
            out_shape=[jax.ShapeDtypeStruct((rows, width), out)] * sides,
            compiler_params=pltpu.CompilerParams(vmem_limit_bytes=48 * MIB),
            cost_estimate=pl.CostEstimate(
                flops=2 * sides * rows * deep * count * width,
                bytes_accessed=2 * deep * count * (sides * rows + width) + 4 * sides * rows * width,
                transcendentals=0,
            ),
            name="blocks_dot",
        )(blocks, *[left for left in lefts for _ in range(count)], *arrays, *added)
    )


def shards(outer_weights, inner_weights, momentum, tokens):
    inner = inner_weights[0]
    token_rows = tokens[0]
    rows, columns = inner.shape
    part = rows // REP
    rep = lax.axis_index("rep")
    core = lax.axis_index("fsdp") % CORE
    chip = lax.axis_index("fsdp") // CORE
    y, x = chip // X, chip % X
    width = token_rows.shape[1]

    def chips_of(moves):
        return jnp.stack([((y + dy) % YH) * X + (x + dx) % X for dy, dx in moves]).astype(jnp.int32)

    early = slice(MAIN, MAIN + EARLY_WIDE)
    yl = (rep // Z).astype(jnp.int32)

    recv = lax.all_to_all(inner.reshape(REP, part, columns), "rep", 0, 0)
    their_tokens = fsdp_move(token_rows, dc=1)
    mine = inner[:, early]
    there, left, right, across = (fsdp_move(mine, *to) for to in ((1, 0), (0, 1), (0, -1), (0, 2)))
    outer_part = lax.dynamic_slice(outer_weights, (rep * part, 0), (part, columns))
    there_left, there_right, there_across = (fsdp_move(there, 0, dx) for dx in (1, -1, 2))
    outer_part = after(outer_part, there, left, right, across, there_left, there_right, there_across)
    momentum_part = lax.dynamic_slice(momentum, (rep * part, MAIN), (part, EARLY_WIDE))
    copies, outer_slice, mean = average_slice(recv, outer_part, momentum_part)
    average = lax.all_to_all(copies, "rep", 0, 0).reshape(rows, MAIN)

    inners = [mine, there, left, there_left, right, there_right, across, there_across]
    pair = jnp.stack([outer_slice, fsdp_move(outer_slice, dy=1)])
    slices = jnp.concatenate(
        [pair, fsdp_move(pair, dx=1), fsdp_move(pair, dx=-1), fsdp_move(pair, dx=2), mean[None]]
    )
    slices = jnp.stack([slices, swap_yl(slices)])
    slices = jnp.broadcast_to(slices[None], (Z, *slices.shape))
    outer_main, momentum_main = update(outer_weights[:, :MAIN], momentum[:, :MAIN], average.astype(F32))
    mixed = mix(inner[:, :MAIN], outer_main)
    late = lax.all_to_all(slices, "rep", 0, 0, axis_index_groups=SAME_YL)

    both = [their_tokens, token_rows]

    def dot(chips, pieces, start=None, lefts=both, out=F32):
        return blocks_dot(lefts, CORE * chips_of(chips) + core, pieces, start, out)

    left, right, there = fsdp_move(mixed, dx=1), fsdp_move(mixed, dx=-1), fsdp_move(mixed, dy=1)
    there_left, there_right, across = fsdp_move(there, dx=1), fsdp_move(there, dx=-1), fsdp_move(left, dx=1)
    sums = dot(NEAR, [(mixed,), (left,), (right,), (there,)])
    there_right = after(there_right, sums[0])
    there_across = fsdp_move(there_right, dx=-1)
    sums = dot(SIDES, [(there_left,), (there_right,)], sums)

    mixed_early, outer_early, average_early = mix_early(inners, after(late, sums[0]), yl)
    pieces = [(mixed_early, k) for k in range(CHIPS)]
    theirs_early = fsdp_move(dot(ORDER, pieces, lefts=both[:1], out=BF16)[0], dc=1)
    ours_early = dot(ORDER, pieces, lefts=both[1:])[0]
    momentum_early = 0.9 * momentum[:, early] + average_early.astype(F32)
    outer_next = jnp.concatenate([outer_main, outer_early], axis=1)
    momentum_next = jnp.concatenate([momentum_main, momentum_early], axis=1)

    last = [(across,), (there_across,)]
    theirs = fsdp_move(dot(LAST, last, sums[:1], both[:1], BF16)[0], dc=1)
    ours = dot(LAST, last, sums[1:], both[1:])[0]
    scale = width ** (-0.5)
    keys = [((o + t.astype(F32)) * scale).astype(BF16) for o, t in ((ours, theirs), (ours_early, theirs_early))]
    return outer_next, momentum_next, jnp.concatenate(keys, axis=1)[None]


def solution(mesh):
    placed = (P("fsdp", None), P("rep", "fsdp", None), P("fsdp", None), P("rep", "fsdp", None))
    return jax.shard_map(
        shards,
        mesh=mesh,
        in_specs=placed,
        out_specs=(P("fsdp", None), P("fsdp", None), P("rep", "fsdp", None)),
        check_vma=False,
    )
```

```python
import jax
import jax.numpy as jnp
from jax import lax
from jax.experimental import pallas as pl
from jax.experimental.pallas import tpu as pltpu
from jax.sharding import PartitionSpec as P

YH, X, CORE = 2, 4, 2
CHIPS = YH * X
REP = 16
MAIN, EARLY_WIDE = 768, 256
NEAR = ((0, 0), (0, -1), (0, 1), (1, 0))
SIDES = ((1, -1), (1, 1))
LAST = ((0, 2), (1, 2))
ORDER = tuple((dy, dx) for dx in (0, -1, 1, 2) for dy in range(YH))
MIB = 1 << 20
F32, BF16 = jnp.float32, jnp.bfloat16
YL, Z = 2, 8
SAME_YL = [[yl * Z + z for z in range(Z)] for yl in range(YL)]


def fsdp_move(array, dy=0, dx=0, dc=0):
    perm = []
    for y in range(YH):
        for x in range(X):
            for c in range(CORE):
                to = (((y + dy) % YH) * X + (x + dx) % X) * CORE + (c + dc) % CORE
                perm.append(((y * X + x) * CORE + c, to))
    return lax.ppermute(array, "fsdp", perm)


def swap_yl(array):
    return lax.ppermute(array, "rep", [(r, (r + Z) % REP) for r in range(REP)])


def to_all_replicas(array):
    return lax.all_to_all(jnp.broadcast_to(array[None], (REP, *array.shape)), "rep", 0, 0)


def after(array, *others):
    def kernel(*refs):
        pass

    space = pl.BlockSpec(memory_space=pl.ANY)
    return pl.pallas_call(
        kernel,
        in_specs=[space] * (1 + len(others)),
        out_specs=space,
        out_shape=jax.ShapeDtypeStruct(array.shape, array.dtype),
        input_output_aliases={0: 0},
        name="after",
    )(array, *others)


def update(outer, moment, average):
    momentum_next = 0.9 * moment + average
    return (outer.astype(F32) - 0.7 * (average + 0.9 * momentum_next)).astype(BF16), momentum_next


def average_slice(recv, outer_rows, momentum_rows):
    replicas, rows, columns = recv.shape

    def kernel(recv_ref, outer_ref, momentum_ref, copies_ref, early_ref, mean_ref):
        for first in range(0, columns, 128):
            cols = slice(first, first + 128)
            outer = outer_ref[:, cols].astype(F32)
            total = jnp.zeros((rows, 128), F32)
            for r in range(replicas):
                delta = outer - recv_ref[r, :, cols].astype(F32)
                scale = jnp.max(jnp.abs(delta), axis=1, keepdims=True) + 1e-6
                quant = (delta / scale).astype(BF16)
                total = total + quant.astype(F32) * scale
            mean = total / replicas
            if first < MAIN:
                for r in range(replicas):
                    copies_ref[r, :, cols] = mean.astype(BF16)
            else:
                cols = slice(first - MAIN, first - MAIN + 128)
                mean_ref[:, cols] = mean.astype(BF16)
                early_ref[:, cols] = update(outer, momentum_ref[:, cols], mean)[0]

    return pl.pallas_call(
        kernel,
        out_shape=[
            jax.ShapeDtypeStruct((replicas, rows, MAIN), BF16),
            jax.ShapeDtypeStruct((rows, columns - MAIN), BF16),
            jax.ShapeDtypeStruct((rows, columns - MAIN), BF16),
        ],
        cost_estimate=pl.CostEstimate(
            flops=10 * replicas * rows * columns, bytes_accessed=4 * replicas * rows * columns, transcendentals=0
        ),
        name="average_slice",
    )(recv, outer_rows, momentum_rows)


def mix(one, other):
    return (0.5 * one.astype(F32) + 0.5 * other.astype(F32)).astype(BF16)


def early_dot(lefts, blocks, inners, late, yl):
    count, (rows, wide) = len(inners), inners[0].shape
    half, tile, sides = rows // YL, 256, len(lefts)
    steps = rows // tile
    lates = YL * (count + 1)

    def kernel(place_ref, *refs):
        tokens, refs = refs[: sides * count], refs[sides * count :]
        outer_ref, average_ref, mixed_ref = refs[-3:]
        outs = refs[-3 - sides : -3]
        step = pl.program_id(0)

        @pl.when(step == 0)
        def _():
            for h in range(YL):
                at = slice(h * half, h * half + half)
                outers = [r[...].reshape(half, wide) for r in refs[count + h * (count + 1) :][: count + 1]]
                for k in range(count):
                    mixed_ref[k, at] = mix(refs[k][at], outers[k])
                outer_ref[at] = outers[0]
                average_ref[at] = outers[count]

        for side in range(sides):

            @pl.when(step // steps == side)
            def _(side=side):
                total = jnp.zeros((tile, wide), F32)
                for k in range(count):
                    total = total + jnp.dot(
                        tokens[side * count + k][...], mixed_ref[k], preferred_element_type=F32
                    )
                outs[side][...] = total.astype(outs[side].dtype)

    def row(side, i):
        return jnp.clip(i - side * steps, 0, steps - 1)

    def left_spec(side, k):
        return pl.BlockSpec((tile, rows), lambda i, place: (row(side, i), place[1 + k]))

    def late_spec(h, k):
        return pl.BlockSpec((Z, None, None, rows // REP, wide), lambda i, place: (0, (place[0] + h) % YL, k, 0, 0))

    def whole(*shape):
        return pl.BlockSpec(shape, lambda i, place: (0,) * len(shape))

    def row_spec(side):
        return pl.BlockSpec((tile, wide), lambda i, place: (row(side, i), 0))

    return pl.pallas_call(
        kernel,
        grid_spec=pltpu.PrefetchScalarGridSpec(
            num_scalar_prefetch=1,
            grid=(sides * steps,),
            in_specs=[left_spec(side, k) for side in range(sides) for k in range(count)]
            + [whole(rows, wide)] * count
            + [late_spec(h, k) for h in range(YL) for k in range(count + 1)],
            out_specs=[row_spec(side) for side in range(sides)] + [whole(rows, wide)] * 2,
            scratch_shapes=[pltpu.VMEM((count, rows, wide), BF16)],
        ),
        out_shape=[jax.ShapeDtypeStruct((rows, wide), dtype) for dtype in (BF16, F32)]
        + [jax.ShapeDtypeStruct((rows, wide), BF16)] * 2,
        compiler_params=pltpu.CompilerParams(vmem_limit_bytes=60 * MIB),
        cost_estimate=pl.CostEstimate(
            flops=2 * sides * rows * rows * count * wide,
            bytes_accessed=2 * rows * count * (sides * rows + 3 * wide),
            transcendentals=0,
        ),
        name="early_dot",
    )(
        jnp.concatenate([yl[None], blocks]),
        *[left for left in lefts for _ in range(count)],
        *inners,
        *([late] * lates),
    )


def blocks_dot(lefts, blocks, pieces, start=None, out=F32):
    rows, tile = lefts[0].shape[0], 256 * len(lefts)
    steps = rows // tile
    count, sides = len(pieces), len(lefts)
    arrays = []
    for piece in pieces:
        if not any(piece[0] is a for a in arrays):
            arrays.append(piece[0])
    found = [next(i for i, a in enumerate(arrays) if a is piece[0]) for piece in pieces]
    deep, width = arrays[0].shape[-2:]
    added = list(start) if start else []

    def kernel(at_ref, *refs):
        rights = refs[sides * count : sides * count + len(arrays)]
        starts = refs[sides * count + len(arrays) : -sides]
        step = pl.program_id(0)
        for side in range(sides):

            @pl.when(step // steps == side)
            def _(side=side):
                total = starts[side][...] if starts else jnp.zeros((tile, width), F32)
                for k, piece in enumerate(pieces):
                    right = rights[found[k]]
                    right = right[piece[1]] if len(piece) > 1 else right[...]
                    total = total + jnp.dot(refs[side * count + k][...], right, preferred_element_type=F32)
                refs[side - sides][...] = total.astype(out)

    def row(side, i):
        return jnp.clip(i - side * steps, 0, steps - 1)

    def left_spec(side, k):
        return pl.BlockSpec((tile, deep), lambda i, at: (row(side, i), at[k]))

    def row_spec(side):
        return pl.BlockSpec((tile, width), lambda i, at: (row(side, i), 0))

    def whole(array):
        return pl.BlockSpec(array.shape, lambda i, at: (0,) * array.ndim)

    return list(
        pl.pallas_call(
            kernel,
            grid_spec=pltpu.PrefetchScalarGridSpec(
                num_scalar_prefetch=1,
                grid=(sides * steps,),
                in_specs=[left_spec(side, k) for side in range(sides) for k in range(count)]
                + [whole(a) for a in arrays]
                + [row_spec(side) for side in range(len(added))],
                out_specs=[row_spec(side) for side in range(sides)],
            ),
            out_shape=[jax.ShapeDtypeStruct((rows, width), out)] * sides,
            compiler_params=pltpu.CompilerParams(vmem_limit_bytes=48 * MIB),
            cost_estimate=pl.CostEstimate(
                flops=2 * sides * rows * deep * count * width,
                bytes_accessed=2 * deep * count * (sides * rows + width) + 4 * sides * rows * width,
                transcendentals=0,
            ),
            name="blocks_dot",
        )(blocks, *[left for left in lefts for _ in range(count)], *arrays, *added)
    )


def shards(outer_weights, inner_weights, momentum, tokens):
    inner = inner_weights[0]
    token_rows = tokens[0]
    rows, columns = inner.shape
    part = rows // REP
    rep = lax.axis_index("rep")
    core = lax.axis_index("fsdp") % CORE
    chip = lax.axis_index("fsdp") // CORE
    y, x = chip // X, chip % X
    width = token_rows.shape[1]

    def chips_of(moves):
        return jnp.stack([((y + dy) % YH) * X + (x + dx) % X for dy, dx in moves]).astype(jnp.int32)

    early = slice(MAIN, MAIN + EARLY_WIDE)
    yl = (rep // Z).astype(jnp.int32)

    recv = lax.all_to_all(inner.reshape(REP, part, columns), "rep", 0, 0)
    their_tokens = fsdp_move(token_rows, dc=1)
    mine = inner[:, early]
    there, left, right, across = (fsdp_move(mine, *to) for to in ((1, 0), (0, 1), (0, -1), (0, 2)))
    outer_part = lax.dynamic_slice(outer_weights, (rep * part, 0), (part, columns))
    there_left, there_right, there_across = (fsdp_move(there, 0, dx) for dx in (1, -1, 2))
    outer_part = after(outer_part, there, left, right, across, there_left, there_right, there_across)
    momentum_part = lax.dynamic_slice(momentum, (rep * part, MAIN), (part, EARLY_WIDE))
    copies, outer_slice, mean = average_slice(recv, outer_part, momentum_part)
    average = lax.all_to_all(copies, "rep", 0, 0).reshape(rows, MAIN)

    inners = [mine, there, left, there_left, right, there_right, across, there_across]
    pair = jnp.stack([outer_slice, fsdp_move(outer_slice, dy=1)])
    slices = jnp.concatenate(
        [pair, fsdp_move(pair, dx=1), fsdp_move(pair, dx=-1), fsdp_move(pair, dx=2), mean[None]]
    )
    slices = jnp.stack([slices, swap_yl(slices)])
    slices = jnp.broadcast_to(slices[None], (Z, *slices.shape))
    outer_main, momentum_main = update(outer_weights[:, :MAIN], momentum[:, :MAIN], average.astype(F32))
    mixed = mix(inner[:, :MAIN], outer_main)
    late = lax.all_to_all(slices, "rep", 0, 0, axis_index_groups=SAME_YL)

    both = [their_tokens, token_rows]

    def dot(chips, pieces, start=None, lefts=both, out=F32):
        return blocks_dot(lefts, CORE * chips_of(chips) + core, pieces, start, out)

    left, right, there = fsdp_move(mixed, dx=1), fsdp_move(mixed, dx=-1), fsdp_move(mixed, dy=1)
    there_left, there_right, across = fsdp_move(there, dx=1), fsdp_move(there, dx=-1), fsdp_move(left, dx=1)
    sums = dot(NEAR, [(mixed,), (left,), (right,), (there,)])
    there_right = after(there_right, sums[0])
    there_across = fsdp_move(there_right, dx=-1)
    sums = dot(SIDES, [(there_left,), (there_right,)], sums)

    theirs_early, ours_early, outer_early, average_early = early_dot(
        both, CORE * chips_of(ORDER) + core, inners, after(late, sums[0]), yl
    )
    theirs_early = fsdp_move(theirs_early, dc=1)
    momentum_early = 0.9 * momentum[:, early] + average_early.astype(F32)
    outer_next = jnp.concatenate([outer_main, outer_early], axis=1)
    momentum_next = jnp.concatenate([momentum_main, momentum_early], axis=1)

    last = [(across,), (there_across,)]
    theirs = fsdp_move(dot(LAST, last, sums[:1], both[:1], BF16)[0], dc=1)
    ours = dot(LAST, last, sums[1:], both[1:])[0]
    scale = width ** (-0.5)
    keys = [((o + t.astype(F32)) * scale).astype(BF16) for o, t in ((ours, theirs), (ours_early, theirs_early))]
    return outer_next, momentum_next, jnp.concatenate(keys, axis=1)[None]


def solution(mesh):
    placed = (P("fsdp", None), P("rep", "fsdp", None), P("fsdp", None), P("rep", "fsdp", None))
    return jax.shard_map(
        shards,
        mesh=mesh,
        in_specs=placed,
        out_specs=(P("fsdp", None), P("fsdp", None), P("rep", "fsdp", None)),
        check_vma=False,
    )
```

```python
import jax
import jax.numpy as jnp
from jax import lax
from jax.experimental import pallas as pl
from jax.experimental.pallas import tpu as pltpu
from jax.sharding import PartitionSpec as P

YH, X, CORE = 2, 4, 2
CHIPS = YH * X
REP = 16
MAIN, EARLY_WIDE = 768, 256
NEAR = ((0, 0), (0, -1), (0, 1), (1, 0))
SIDES = ((1, -1), (1, 1))
LAST = ((0, 2), (1, 2))
ORDER = tuple((dy, dx) for dx in (0, -1, 1, 2) for dy in range(YH))
MIB = 1 << 20
F32, BF16 = jnp.float32, jnp.bfloat16
YL, Z = 2, 8
SAME_YL = [[yl * Z + z for z in range(Z)] for yl in range(YL)]


def fsdp_move(array, dy=0, dx=0, dc=0):
    perm = []
    for y in range(YH):
        for x in range(X):
            for c in range(CORE):
                to = (((y + dy) % YH) * X + (x + dx) % X) * CORE + (c + dc) % CORE
                perm.append(((y * X + x) * CORE + c, to))
    return lax.ppermute(array, "fsdp", perm)


def swap_yl(array):
    return lax.ppermute(array, "rep", [(r, (r + Z) % REP) for r in range(REP)])


def to_all_replicas(array):
    return lax.all_to_all(jnp.broadcast_to(array[None], (REP, *array.shape)), "rep", 0, 0)


def after(array, *others):
    def kernel(*refs):
        pass

    space = pl.BlockSpec(memory_space=pl.ANY)
    return pl.pallas_call(
        kernel,
        in_specs=[space] * (1 + len(others)),
        out_specs=space,
        out_shape=jax.ShapeDtypeStruct(array.shape, array.dtype),
        input_output_aliases={0: 0},
        name="after",
    )(array, *others)


def update(outer, moment, average):
    momentum_next = 0.9 * moment + average
    return (outer.astype(F32) - 0.7 * (average + 0.9 * momentum_next)).astype(BF16), momentum_next


def average_slice(recv, outer_rows, momentum_rows):
    replicas, rows, columns = recv.shape

    def kernel(recv_ref, outer_ref, momentum_ref, copies_ref, early_ref, mean_ref):
        for first in range(0, columns, 128):
            cols = slice(first, first + 128)
            outer = outer_ref[:, cols].astype(F32)
            total = jnp.zeros((rows, 128), F32)
            for r in range(replicas):
                delta = outer - recv_ref[r, :, cols].astype(F32)
                scale = jnp.max(jnp.abs(delta), axis=1, keepdims=True) + 1e-6
                quant = (delta / scale).astype(BF16)
                total = total + quant.astype(F32) * scale
            mean = total / replicas
            if first < MAIN:
                for r in range(replicas):
                    copies_ref[r, :, cols] = mean.astype(BF16)
            else:
                cols = slice(first - MAIN, first - MAIN + 128)
                mean_ref[:, cols] = mean.astype(BF16)
                early_ref[:, cols] = update(outer, momentum_ref[:, cols], mean)[0]

    return pl.pallas_call(
        kernel,
        out_shape=[
            jax.ShapeDtypeStruct((replicas, rows, MAIN), BF16),
            jax.ShapeDtypeStruct((rows, columns - MAIN), BF16),
            jax.ShapeDtypeStruct((rows, columns - MAIN), BF16),
        ],
        cost_estimate=pl.CostEstimate(
            flops=10 * replicas * rows * columns, bytes_accessed=4 * replicas * rows * columns, transcendentals=0
        ),
        name="average_slice",
    )(recv, outer_rows, momentum_rows)


def mix(one, other):
    return (0.5 * one.astype(F32) + 0.5 * other.astype(F32)).astype(BF16)


def early_dot(lefts, blocks, inners, late, yl, momentum):
    count, (rows, wide) = len(inners), inners[0].shape
    half, tile, sides = rows // YL, 256, len(lefts)
    steps = rows // tile
    lates = YL * (count + 1)

    def kernel(place_ref, *refs):
        tokens, refs = refs[: sides * count], refs[sides * count :]
        outer_ref, momentum_next_ref, mixed_ref = refs[-3:]
        momentum_ref = refs[count + lates]
        outs = refs[-3 - sides : -3]
        step = pl.program_id(0)

        @pl.when(step == 0)
        def _():
            for h in range(YL):
                at = slice(h * half, h * half + half)
                outers = [r[...].reshape(half, wide) for r in refs[count + h * (count + 1) :][: count + 1]]
                for k in range(count):
                    mixed_ref[k, at] = mix(refs[k][at], outers[k])
                outer_ref[at] = outers[0]
                momentum_next_ref[at] = 0.9 * momentum_ref[at] + outers[count].astype(F32)

        for side in range(sides):

            @pl.when(step // steps == side)
            def _(side=side):
                total = jnp.zeros((tile, wide), F32)
                for k in range(count):
                    total = total + jnp.dot(
                        tokens[side * count + k][...], mixed_ref[k], preferred_element_type=F32
                    )
                outs[side][...] = total.astype(outs[side].dtype)

    def row(side, i):
        return jnp.clip(i - side * steps, 0, steps - 1)

    def left_spec(side, k):
        return pl.BlockSpec((tile, rows), lambda i, place: (row(side, i), place[1 + k]))

    def late_spec(h, k):
        return pl.BlockSpec((Z, None, None, rows // REP, wide), lambda i, place: (0, (place[0] + h) % YL, k, 0, 0))

    def whole(*shape):
        return pl.BlockSpec(shape, lambda i, place: (0,) * len(shape))

    def row_spec(side):
        return pl.BlockSpec((tile, wide), lambda i, place: (row(side, i), 0))

    return pl.pallas_call(
        kernel,
        grid_spec=pltpu.PrefetchScalarGridSpec(
            num_scalar_prefetch=1,
            grid=(sides * steps,),
            in_specs=[left_spec(side, k) for side in range(sides) for k in range(count)]
            + [whole(rows, wide)] * count
            + [late_spec(h, k) for h in range(YL) for k in range(count + 1)]
            + [pl.BlockSpec((rows, wide), lambda i, place: (0, MAIN // wide))],
            out_specs=[row_spec(side) for side in range(sides)] + [whole(rows, wide)] * 2,
            scratch_shapes=[pltpu.VMEM((count, rows, wide), BF16)],
        ),
        out_shape=[jax.ShapeDtypeStruct((rows, wide), dtype) for dtype in (BF16, F32)]
        + [jax.ShapeDtypeStruct((rows, wide), dtype) for dtype in (BF16, F32)],
        compiler_params=pltpu.CompilerParams(vmem_limit_bytes=60 * MIB),
        cost_estimate=pl.CostEstimate(
            flops=2 * sides * rows * rows * count * wide,
            bytes_accessed=2 * rows * count * (sides * rows + 3 * wide),
            transcendentals=0,
        ),
        name="early_dot",
    )(
        jnp.concatenate([yl[None], blocks]),
        *[left for left in lefts for _ in range(count)],
        *inners,
        *([late] * lates),
        momentum,
    )


def blocks_dot(lefts, blocks, pieces, start=None, out=F32):
    rows, tile = lefts[0].shape[0], 256 * len(lefts)
    steps = rows // tile
    count, sides = len(pieces), len(lefts)
    arrays = []
    for piece in pieces:
        if not any(piece[0] is a for a in arrays):
            arrays.append(piece[0])
    found = [next(i for i, a in enumerate(arrays) if a is piece[0]) for piece in pieces]
    deep, width = arrays[0].shape[-2:]
    added = list(start) if start else []

    def kernel(at_ref, *refs):
        rights = refs[sides * count : sides * count + len(arrays)]
        starts = refs[sides * count + len(arrays) : -sides]
        step = pl.program_id(0)
        for side in range(sides):

            @pl.when(step // steps == side)
            def _(side=side):
                total = starts[side][...] if starts else jnp.zeros((tile, width), F32)
                for k, piece in enumerate(pieces):
                    right = rights[found[k]]
                    right = right[piece[1]] if len(piece) > 1 else right[...]
                    total = total + jnp.dot(refs[side * count + k][...], right, preferred_element_type=F32)
                refs[side - sides][...] = total.astype(out)

    def row(side, i):
        return jnp.clip(i - side * steps, 0, steps - 1)

    def left_spec(side, k):
        return pl.BlockSpec((tile, deep), lambda i, at: (row(side, i), at[k]))

    def row_spec(side):
        return pl.BlockSpec((tile, width), lambda i, at: (row(side, i), 0))

    def whole(array):
        return pl.BlockSpec(array.shape, lambda i, at: (0,) * array.ndim)

    return list(
        pl.pallas_call(
            kernel,
            grid_spec=pltpu.PrefetchScalarGridSpec(
                num_scalar_prefetch=1,
                grid=(sides * steps,),
                in_specs=[left_spec(side, k) for side in range(sides) for k in range(count)]
                + [whole(a) for a in arrays]
                + [row_spec(side) for side in range(len(added))],
                out_specs=[row_spec(side) for side in range(sides)],
            ),
            out_shape=[jax.ShapeDtypeStruct((rows, width), out)] * sides,
            compiler_params=pltpu.CompilerParams(vmem_limit_bytes=48 * MIB),
            cost_estimate=pl.CostEstimate(
                flops=2 * sides * rows * deep * count * width,
                bytes_accessed=2 * deep * count * (sides * rows + width) + 4 * sides * rows * width,
                transcendentals=0,
            ),
            name="blocks_dot",
        )(blocks, *[left for left in lefts for _ in range(count)], *arrays, *added)
    )


def shards(outer_weights, inner_weights, momentum, tokens):
    inner = inner_weights[0]
    token_rows = tokens[0]
    rows, columns = inner.shape
    part = rows // REP
    rep = lax.axis_index("rep")
    core = lax.axis_index("fsdp") % CORE
    chip = lax.axis_index("fsdp") // CORE
    y, x = chip // X, chip % X
    width = token_rows.shape[1]

    def chips_of(moves):
        return jnp.stack([((y + dy) % YH) * X + (x + dx) % X for dy, dx in moves]).astype(jnp.int32)

    early = slice(MAIN, MAIN + EARLY_WIDE)
    yl = (rep // Z).astype(jnp.int32)

    recv = lax.all_to_all(inner.reshape(REP, part, columns), "rep", 0, 0)
    their_tokens = fsdp_move(token_rows, dc=1)
    mine = inner[:, early]
    there, left, right, across = (fsdp_move(mine, *to) for to in ((1, 0), (0, 1), (0, -1), (0, 2)))
    outer_part = lax.dynamic_slice(outer_weights, (rep * part, 0), (part, columns))
    there_left, there_right, there_across = (fsdp_move(there, 0, dx) for dx in (1, -1, 2))
    outer_part = after(outer_part, there, left, right, across, there_left, there_right, there_across)
    momentum_part = lax.dynamic_slice(momentum, (rep * part, MAIN), (part, EARLY_WIDE))
    copies, outer_slice, mean = average_slice(recv, outer_part, momentum_part)
    average = lax.all_to_all(copies, "rep", 0, 0).reshape(rows, MAIN)

    inners = [mine, there, left, there_left, right, there_right, across, there_across]
    pair = jnp.stack([outer_slice, fsdp_move(outer_slice, dy=1)])
    slices = jnp.concatenate(
        [pair, fsdp_move(pair, dx=1), fsdp_move(pair, dx=-1), fsdp_move(pair, dx=2), mean[None]]
    )
    slices = jnp.stack([slices, swap_yl(slices)])
    slices = jnp.broadcast_to(slices[None], (Z, *slices.shape))
    outer_main, momentum_main = update(outer_weights[:, :MAIN], momentum[:, :MAIN], average.astype(F32))
    mixed = mix(inner[:, :MAIN], outer_main)
    late = lax.all_to_all(slices, "rep", 0, 0, axis_index_groups=SAME_YL)

    both = [their_tokens, token_rows]

    def dot(chips, pieces, start=None, lefts=both, out=F32):
        return blocks_dot(lefts, CORE * chips_of(chips) + core, pieces, start, out)

    left, right, there = fsdp_move(mixed, dx=1), fsdp_move(mixed, dx=-1), fsdp_move(mixed, dy=1)
    there_left, there_right, across = fsdp_move(there, dx=1), fsdp_move(there, dx=-1), fsdp_move(left, dx=1)
    sums = dot(NEAR, [(mixed,), (left,), (right,), (there,)])
    there_right = after(there_right, sums[0])
    there_across = fsdp_move(there_right, dx=-1)
    sums = dot(SIDES, [(there_left,), (there_right,)], sums)

    theirs_early, ours_early, outer_early, momentum_early = early_dot(
        both, CORE * chips_of(ORDER) + core, inners, after(late, sums[0]), yl, momentum
    )
    theirs_early = fsdp_move(theirs_early, dc=1)
    outer_next = jnp.concatenate([outer_main, outer_early], axis=1)
    momentum_next = jnp.concatenate([momentum_main, momentum_early], axis=1)

    last = [(across,), (there_across,)]
    theirs = fsdp_move(dot(LAST, last, sums[:1], both[:1], BF16)[0], dc=1)
    ours = dot(LAST, last, sums[1:], both[1:])[0]
    scale = width ** (-0.5)
    keys = [((o + t.astype(F32)) * scale).astype(BF16) for o, t in ((ours, theirs), (ours_early, theirs_early))]
    return outer_next, momentum_next, jnp.concatenate(keys, axis=1)[None]


def solution(mesh):
    placed = (P("fsdp", None), P("rep", "fsdp", None), P("fsdp", None), P("rep", "fsdp", None))
    return jax.shard_map(
        shards,
        mesh=mesh,
        in_specs=placed,
        out_specs=(P("fsdp", None), P("fsdp", None), P("rep", "fsdp", None)),
        check_vma=False,
    )
```
